32 devices in a mesh: groups: 2 (over y), ctx: 16 (over z, x, core).
Axes of the slice: x: 2, y: 2, z: 4, core: 2. Of those that a mesh axis runs over, the one named last changes fastest.
Arguments:
- queries: bfloat16 [4096, 512], P(('groups', 'ctx')), parts along dimension 0, may hold values from -51 to 51
- keys: bfloat16 [4096, 128], P(('groups', 'ctx')), parts along dimension 0, may hold values from -6 to 6
- values: bfloat16 [4096, 128], P(('groups', 'ctx')), parts along dimension 0, may hold values from -6 to 6
- grad_out: bfloat16 [4096, 512], P(('groups', 'ctx')), parts along dimension 0, may hold values from -24 to 24
- key_blocks: int32 [32, 8], P('groups'), parts along dimension 0, may hold values from 0 to 15, as said below
- key_counts: int32 [32], P('groups'), parts along dimension 0, may hold values from 1 to 8, as said below
- block_slot: int32 [32], P('groups'), parts along dimension 0, may hold values from 0 to 15, each once
Outputs:
- attended: bfloat16 [4096, 512], P(('groups', 'ctx')), parts along dimension 0
- grad_queries: bfloat16 [4096, 512], P(('groups', 'ctx')), parts along dimension 0
- grad_keys: bfloat16 [4096, 128], P(('groups', 'ctx')), parts along dimension 0
- grad_values: bfloat16 [4096, 128], P(('groups', 'ctx')), parts along dimension 0
The draws below stay inside these ranges and needn't reach their ends.
There are 2 independent parts, one for each index of `groups`. The reference program is written for one: setup_inputs(seed, part) draws one part's arguments, and reference() takes and returns one part's arrays. A program takes and returns all parts, laid end to end along the dimension named above; each array names one. Nothing has to cross between parts.
Inputs may be any that keep to these rules, and one draw needn't show every extreme that they name: `key_blocks`: row b: its first key_counts[b] entries are distinct sequence blocks of 0 to b, the first entry being b itself; every later entry equals b. key_counts[b] <= b + 1; the last block's count is 8.
All inputs are finite; a program needn't handle non-finite values.
Results may differ from the reference program's by a relative error of at most 0.017.
Values may be sent and summed in bfloat16 or wider, within the bound.
A program may use at most 128 MiB of HBM per device.

```python
import math
import jax
import jax.numpy as jnp
from jax import lax

HD = 128
QH = 4
BLK = 128
SEQ = 2048
NBLK = 16
KMAX = 8


def list_draw(key):
    count_key = jax.random.fold_in(key, 101)
    order_key = jax.random.fold_in(key, 102)
    blocks = jnp.arange(NBLK, dtype=jnp.int32)
    drawn_counts = jax.random.randint(count_key, (NBLK,), KMAX // 4, KMAX + 1, dtype=jnp.int32)
    counts = jnp.minimum(drawn_counts, blocks + 1)
    counts = jnp.where(blocks == NBLK - 1, KMAX, counts)
    rank_values = jax.random.randint(order_key, (NBLK, NBLK), 0, 1 << 18, dtype=jnp.int32)
    earlier = blocks[None, :] < blocks[:, None]
    rank_values = jnp.where(earlier, rank_values, 1 << 18) * NBLK + blocks[None, :]
    chosen = jnp.argsort(rank_values, axis=1, stable=True).astype(jnp.int32)[:, :KMAX - 1]
    block_lists = jnp.concatenate([blocks[:, None], chosen], axis=1)
    slot_index = jnp.arange(KMAX, dtype=jnp.int32)[None, :]
    block_lists = jnp.where(slot_index < counts[:, None], block_lists, blocks[:, None])
    return (block_lists, counts)


def draw_key_blocks(key, part):
    return list_draw(key)[0]


def draw_key_counts(key, part):
    return list_draw(key)[1]


def key_field(key):
    base_key = jax.random.fold_in(key, 201)
    field = jnp.clip(jax.random.normal(base_key, (SEQ, HD), jnp.float32), -6.0, 6.0)
    return field


def draw_keys(key, part):
    return key_field(key).astype(jnp.bfloat16)


def draw_queries(key, part):
    query_key = jax.random.fold_in(key, 301)
    column_total = QH * HD
    field = 2.5 * jnp.clip(jax.random.normal(query_key, (SEQ, column_total), jnp.float32), -6.0, 6.0)
    return field.astype(jnp.bfloat16)


def block_levels(stream_key, dims, cuts, smallest, high):
    def one(axis_at, shards_of):
        draws = jax.random.uniform(jax.random.fold_in(jax.random.fold_in(stream_key, 6), axis_at), (shards_of,), jnp.float32, smallest / len(cuts), high / len(cuts))
        return jnp.repeat(jnp.exp(draws), dims[axis_at] // shards_of).reshape((-1,) + (1,) * (len(dims) - axis_at - 1))

    factor_of = one(*cuts[0])
    for cut in cuts[1:]:
        factor_of = factor_of * one(*cut)
    return factor_of


def gaussian(stream_key, extent, spread, most, cuts=(), kind=jnp.bfloat16):
    gain = block_levels(stream_key, extent, cuts, -0.22, 0.18) if cuts else 1.0
    drawn = jax.random.normal(stream_key, extent, jnp.float32) * spread * gain
    return jnp.minimum(jnp.maximum(drawn, -most), most).astype(kind)


def setup_inputs(seed: int = 0, part: int = 0) -> dict:
    splits = jax.random.split(jax.random.key(seed), 8)
    part_keys = jax.random.split(jax.random.fold_in(splits[7], part), 8)
    return {
        "queries": draw_queries(jax.random.fold_in(jax.random.fold_in(splits[7], part), 71), part),
        "keys": draw_keys(jax.random.fold_in(jax.random.fold_in(splits[7], part), 71), part),
        "values": gaussian(part_keys[2], (SEQ, HD), 1.0, 6.0, ((0, 16),)),
        "grad_out": gaussian(part_keys[3], (SEQ, QH * HD), 4.0, 24.0, ((0, 16),)),
        "key_blocks": draw_key_blocks(jax.random.fold_in(jax.random.fold_in(splits[7], part), 71), part),
        "key_counts": draw_key_counts(jax.random.fold_in(jax.random.fold_in(splits[7], part), 71), part),
        "block_slot": jax.random.permutation(part_keys[6], NBLK).astype(jnp.int32),
    }


NEG_LARGE = -1e+30

def reference(queries, keys, values, grad_out, key_blocks, key_counts, block_slot):
    block_total = key_blocks.shape[0]
    slot_total = key_blocks.shape[1]
    head_dim = keys.shape[1]
    head_count = queries.shape[1] // head_dim
    score_scale = 1.0 / math.sqrt(head_dim)
    key_tiles = keys.reshape(block_total, BLK, head_dim)
    value_tiles = values.reshape(block_total, BLK, head_dim)
    query_tiles = queries.reshape(block_total, BLK * head_count, head_dim)
    grad_tiles = grad_out.reshape(block_total, BLK * head_count, head_dim)
    block_ids = jnp.arange(block_total, dtype=jnp.int32)
    columns = jnp.arange(slot_total * BLK, dtype=jnp.int32)
    slot_of = columns // BLK
    row_token = jnp.arange(BLK * head_count, dtype=jnp.int32) // head_count

    def visit_block(sums, stored_block):
        key_sum, value_sum = sums
        query_block = jnp.sum(jnp.where(block_slot == stored_block, block_ids, 0)).astype(jnp.int32)
        key_list = key_blocks[query_block]
        stored_list = block_slot[key_list]
        key_rows = key_tiles[stored_list].reshape(slot_total * BLK, head_dim)
        value_rows = value_tiles[stored_list].reshape(slot_total * BLK, head_dim)
        query_rows = query_tiles[stored_block]
        grad_rows = grad_tiles[stored_block]
        key_position = key_list[slot_of] * BLK + columns % BLK
        query_position = query_block * BLK + row_token
        allowed = (slot_of < key_counts[query_block])[None, :] & (key_position[None, :] <= query_position[:, None])
        scores = jnp.dot(query_rows, key_rows.T, preferred_element_type=jnp.float32) * score_scale
        masked = jnp.where(allowed, scores, NEG_LARGE)
        row_max = lax.optimization_barrier(jnp.max(masked, axis=1))
        row_sum = lax.optimization_barrier(jnp.sum(jnp.where(allowed, jnp.exp(masked - row_max[:, None]), 0.0), axis=1))
        log_total = row_max + jnp.log(row_sum)
        prob_values = jnp.where(allowed, jnp.exp(scores - log_total[:, None]), 0.0)
        weights = prob_values.astype(jnp.bfloat16)
        attended = jnp.dot(weights, value_rows, preferred_element_type=jnp.float32).astype(jnp.bfloat16)
        row_delta = lax.optimization_barrier(jnp.sum(grad_rows.astype(jnp.float32) * attended.astype(jnp.float32), axis=1))
        dprobs = jnp.dot(grad_rows, value_rows.T, preferred_element_type=jnp.float32)
        dscores = (prob_values * (dprobs - row_delta[:, None])).astype(jnp.bfloat16)
        query_grad = (jnp.dot(dscores, key_rows, preferred_element_type=jnp.float32) * score_scale).astype(jnp.bfloat16)
        key_part = jnp.dot(dscores.T, query_rows, preferred_element_type=jnp.float32) * score_scale
        value_part = jnp.dot(weights.T, grad_rows, preferred_element_type=jnp.float32)
        key_sum = key_sum.at[stored_list].add(key_part.reshape(slot_total, BLK, head_dim))
        value_sum = value_sum.at[stored_list].add(value_part.reshape(slot_total, BLK, head_dim))
        return ((key_sum, value_sum), (attended, query_grad))
    start_sums = (jnp.zeros((block_total, BLK, head_dim), jnp.float32), jnp.zeros((block_total, BLK, head_dim), jnp.float32))
    final_sums, per_block = lax.scan(visit_block, start_sums, block_ids)
    token_total = block_total * BLK
    attended = per_block[0].reshape(token_total, head_count * head_dim)
    grad_queries = per_block[1].reshape(token_total, head_count * head_dim)
    grad_keys = final_sums[0].reshape(token_total, head_dim).astype(jnp.bfloat16)
    grad_values = final_sums[1].reshape(token_total, head_dim).astype(jnp.bfloat16)
    return (attended, grad_queries, grad_keys, grad_values)
```

```python
import functools
import math

import jax
import jax.numpy as jnp
from jax import lax
from jax.experimental import pallas as pl
from jax.experimental.pallas import tpu as pltpu
from jax.sharding import PartitionSpec as P

BLK = 128
NEG = -1e30
F32 = jnp.float32
BF16 = jnp.bfloat16
MESH = pl.DeviceIdType.MESH


def grid_of(device_total):
    chips = device_total // 2
    power = chips.bit_length() - 1
    x_size = 2 ** (power // 3)
    return chips // x_size, x_size


def loop(count, body, most=4):
    if count <= most:
        for step in range(count):
            body(step)
    else:
        lax.fori_loop(0, count, lambda step, _: (body(step), 0)[1], 0)


def dot(a, b, a_dim, b_dim):
    return lax.dot_general(a, b, (((a_dim,), (b_dim,)), ((), ())), preferred_element_type=F32)


def kernel(
    sizes,
    q_ref, k_ref, v_ref, g_ref, lists_ref, counts_ref, slot_ref,
    out_ref, dq_ref, dk_ref, dv_ref,
    kv, q_rows, g_rows, q_cols, g_cols, bias, tri, top, total, acc, dq_acc, tops,
    exps, dprobs, part, from_core, from_x, from_z,
    ag_send, ag_recv, rs_send, rs_recv,
):
    heads, head_dim, z_size, x_size, keep = sizes
    device_total = 2 * x_size * z_size
    lines = 2 * x_size
    rows = heads * BLK
    scale = 1.0 / math.sqrt(head_dim)
    scale2 = scale * math.log2(math.e)
    me = lax.axis_index("ctx")
    group = lax.axis_index("groups")
    c = lax.rem(me, 2)
    x = lax.rem(me // 2, x_size)
    z = me // (2 * x_size)
    other = 1 - c

    def device(zi, xi, ci):
        return (group, (zi * x_size + xi) * 2 + ci)

    def place(z_step, x_step, c_step):
        return (x_step * 2 + c_step) * z_size + z_step

    def tile(block):
        return pl.ds(pl.multiple_of(block * BLK, BLK), BLK)

    def turn_z(step):
        return lax.rem(z + step, z_size)

    def turn_x(step):
        return lax.rem(x + step, x_size)

    mine = 0
    kv[mine, 0] = k_ref[...]
    kv[mine, 1] = v_ref[...]
    barrier = pltpu.get_barrier_semaphore()
    for step in range(1, z_size):
        pl.semaphore_signal(barrier, inc=1, device_id=device(turn_z(step), x, c), device_id_type=MESH)
    for step in range(1, x_size):
        pl.semaphore_signal(barrier, inc=1, device_id=device(z, turn_x(step), c), device_id_type=MESH)
    pl.semaphore_signal(barrier, inc=1, device_id=device(z, x, other), device_id_type=MESH)

    pl.semaphore_wait(barrier, z_size + x_size - 1)

    def share(block, there, where, number):
        return pltpu.make_async_remote_copy(
            src_ref=kv.at[block],
            dst_ref=kv.at[there],
            send_sem=ag_send.at[number],
            recv_sem=ag_recv.at[there],
            device_id=where,
            device_id_type=MESH,
        )

    x_base = z_size - 1
    core_base = x_base + (x_size - 1) * z_size

    def share_z(step):
        return share(mine, place(z_size - step, 0, 0), device(turn_z(step), x, c), step - 1)

    def share_x(x_step, z_step):
        return share(
            place(z_step, 0, 0),
            place(z_step, x_size - x_step, 0),
            device(z, turn_x(x_step), c),
            x_base + (x_step - 1) * z_size + z_step,
        )

    def share_core(x_step, z_step):
        return share(
            place(z_step, x_step, 0),
            place(z_step, x_step, 1),
            device(z, x, other),
            core_base + x_step * z_size + z_step,
        )

    loop(z_size - 1, lambda i: share_z(i + 1).start(), 15)
    loop(x_size - 1, lambda i: share_x(i + 1, 0).start())
    share_core(0, 0).start()

    for h in range(heads):
        cols = slice(h * head_dim, (h + 1) * head_dim)
        q_tile = q_ref[:, cols]
        g_tile = g_ref[:, cols]
        q_rows[h * BLK:(h + 1) * BLK, :] = q_tile
        g_rows[h * BLK:(h + 1) * BLK, :] = g_tile
        q_cols[:, h * BLK:(h + 1) * BLK] = q_tile.T
        g_cols[:, h * BLK:(h + 1) * BLK] = g_tile.T

    block_total, slot_total = lists_ref.shape

    def find(j, found):
        return jnp.where(slot_ref[j] == me, j, found)

    query_block = lax.fori_loop(0, block_total, find, jnp.int32(0))
    count = counts_ref[query_block]
    bias[...] = jnp.full(bias.shape, NEG, F32)
    block_ids = lax.broadcasted_iota(jnp.int32, bias.shape, 0)

    def open_block(k, _):
        stored = slot_ref[lists_ref[query_block, k]]
        c_step = lax.rem(stored + c, 2)
        x_step = lax.rem(stored // 2 - x + lines, x_size)
        z_step = lax.rem(stored // lines - z + z_size, z_size)
        spot = place(z_step, x_step, c_step)
        spot = jnp.where(k < count, spot, -1)
        bias[...] = jnp.where(block_ids == spot, 0.0, bias[...])
        return 0

    lax.fori_loop(0, slot_total, open_block, 0)
    key_at = lax.broadcasted_iota(jnp.int32, (BLK, rows), 0)
    query_at = lax.rem(lax.broadcasted_iota(jnp.int32, (BLK, rows), 1), BLK)
    tri[...] = jnp.where(key_at <= query_at, 0.0, NEG)
    top[...] = jnp.full(top.shape, NEG, F32)
    total[...] = jnp.zeros(total.shape, F32)
    acc[...] = jnp.zeros(acc.shape, F32)
    dq_acc[...] = jnp.zeros(dq_acc.shape, F32)

    def scores_of(block, own):
        raw = dot(kv[block, 0], q_cols[...], 1, 0) * scale2
        return raw + (tri[...] if own else bias[pl.ds(block, 1), :])

    def forward(block, own=False):
        values = kv[block, 1]
        scores = scores_of(block, own)
        old = top[...]
        new = jnp.maximum(old, jnp.max(scores, axis=0, keepdims=True))
        terms = jnp.exp2(scores - new)
        fade = jnp.exp2(old - new)
        top[...] = new
        total[...] = total[...] * fade + jnp.sum(terms, axis=0, keepdims=True)
        acc[...] = acc[...] * fade + dot(values, terms.astype(BF16), 0, 0)
        if keep:
            exps[tile(block), :] = terms
            tops[pl.ds(block, 1), :] = new
            dprobs[tile(block), :] = dot(values, g_cols[...], 1, 0)

    forward(mine, True)

    def take_z(i):
        step = i + 1
        block = place(step, 0, 0)
        share(mine, block, device(z, x, other), 0).wait_recv()
        loop(x_size - 1, lambda j: share_x(j + 1, step).start())
        share_core(0, step).start()

    loop(z_size - 1, take_z)
    loop(z_size - 1, lambda i: forward(place(i + 1, 0, 0)), 0)

    def take_x(x_step):
        def one(step):
            block = place(step, x_step, 0)
            share(mine, block, device(z, x, other), 0).wait_recv()
            share_core(x_step, step).start()

        loop(z_size, one)
        loop(z_size, lambda step: forward(place(step, x_step, 0)), 0)

    loop(x_size - 1, lambda i: take_x(i + 1))

    def take_core(x_step):
        def one(step):
            block = place(step, x_step, 1)
            share(mine, block, device(z, x, other), 0).wait_recv()
            forward(block)

        loop(z_size, one, 0)

    loop(x_size, take_core, 0)

    inverse = 1.0 / total[...]
    attended = (acc[...] * inverse).T.astype(BF16)
    for h in range(heads):
        part_rows = slice(h * BLK, (h + 1) * BLK)
        out_ref[:, h * head_dim:(h + 1) * head_dim] = attended[part_rows, :]
    rounded = (acc[...] * inverse).astype(BF16).astype(F32)
    delta = jnp.sum(g_cols[...].astype(F32) * rounded, axis=0, keepdims=True)
    total[...] = inverse
    acc[0:1, :] = delta

    def backward(block, own=False):
        keys = kv[block, 0]
        if keep:
            probs = exps[tile(block), :] * (
                jnp.exp2(tops[pl.ds(block, 1), :] - top[...]) * total[...]
            )
            dprob = dprobs[tile(block), :]
        else:
            probs = jnp.exp2(scores_of(block, own) - top[...]) * total[...]
            dprob = dot(kv[block, 1], g_cols[...], 1, 0)
        dscores = (probs * (dprob - acc[0:1, :])).astype(BF16)
        dq_acc[...] += dot(keys, dscores, 0, 0)
        dkey = dot(dscores, q_rows[...], 1, 0) * scale
        dvalue = dot(probs.astype(BF16), g_rows[...], 1, 0)
        return dkey, dvalue

    def post(block, pair):
        part[block, 0] = pair[0].astype(BF16)
        part[block, 1] = pair[1].astype(BF16)

    def plus(pair, landed, slot):
        return (
            pair[0] + landed[slot, 0].astype(F32),
            pair[1] + landed[slot, 1].astype(F32),
        )

    def give(block, landed, slot, where, number):
        return pltpu.make_async_remote_copy(
            src_ref=part.at[block],
            dst_ref=landed.at[slot],
            send_sem=rs_send.at[number],
            recv_sem=rs_recv.at[number],
            device_id=where,
            device_id_type=MESH,
        )

    def give_core(x_at, z_at):
        slot = x_at * z_size + z_at
        return give(
            place(z_at, x_at, 1), from_core, slot, device(z, x, other), core_base + slot
        )

    def give_x(x_step, z_at):
        slot = (x_step - 1) * z_size + z_at
        return give(
            place(z_at, x_step, 0), from_x, slot, device(z, turn_x(x_step), c), x_base + slot
        )

    def give_z(z_step):
        return give(
            place(z_step, 0, 0), from_z, z_step - 1, device(turn_z(z_step), x, c), z_step - 1
        )

    def to_core(x_at):
        def one(z_at):
            block = place(z_at, x_at, 1)
            post(block, backward(block))
            give_core(x_at, z_at).start()

        loop(z_size, one, 0)

    def to_x(x_step):
        x_at = x_step

        def one(i):
            z_at = lax.rem(i + 1, z_size)
            block = place(z_at, x_at, 0)
            pair = backward(block)
            give_core(x_at, z_at).wait_recv()
            post(block, plus(pair, from_core, x_at * z_size + z_at))
            give_x(x_step, z_at).start()

        loop(z_size, one, 0)

    def away(i):
        to_core(i + 1)
        to_x(i + 1)

    loop(x_size - 1, away, 1)
    to_core(0)

    def gathered(z_at, own):
        block = place(z_at, 0, 0)
        pair = backward(block, own)
        give_core(0, z_at).wait_recv()
        pair = plus(pair, from_core, z_at)
        for x_step in range(1, x_size):
            give_x(x_step, z_at).wait_recv()
            pair = plus(pair, from_x, (x_step - 1) * z_size + z_at)
        return block, pair

    def to_z(i):
        block, pair = gathered(i + 1, False)
        post(block, pair)
        give_z(i + 1).start()

    loop(z_size - 1, to_z, 0)
    block, pair = gathered(0, True)
    query_grad = (dq_acc[...] * scale).T.astype(BF16)
    for h in range(heads):
        dq_ref[:, h * head_dim:(h + 1) * head_dim] = query_grad[h * BLK:(h + 1) * BLK, :]
    for z_step in range(1, z_size):
        give_z(z_step).wait_recv()
        pair = plus(pair, from_z, z_step - 1)
    dk_ref[...] = pair[0].astype(BF16)
    dv_ref[...] = pair[1].astype(BF16)

    loop(device_total - 1, lambda i: share(mine, mine, device(z, x, other), i).wait_send(), 0)
    loop(
        device_total - 1,
        lambda i: give(mine, from_core, 0, device(z, x, other), i).wait_send(),
        0,
    )


def per_device(queries, keys, values, grad_out, key_blocks, key_counts, block_slot):
    token_rows, width = queries.shape
    head_dim = keys.shape[1]
    heads = width // head_dim
    device_total = key_blocks.shape[0] * BLK // token_rows
    z_size, x_size = grid_of(device_total)
    keep = device_total <= 32
    rows = heads * BLK
    kept = device_total * BLK if keep else 8
    vmem = pl.BlockSpec(memory_space=pltpu.VMEM)
    smem = pl.BlockSpec(memory_space=pltpu.SMEM)
    call = pl.pallas_call(
        functools.partial(kernel, (heads, head_dim, z_size, x_size, keep)),
        out_shape=(
            jax.ShapeDtypeStruct(queries.shape, BF16),
            jax.ShapeDtypeStruct(queries.shape, BF16),
            jax.ShapeDtypeStruct(keys.shape, BF16),
            jax.ShapeDtypeStruct(values.shape, BF16),
        ),
        in_specs=[vmem] * 4 + [smem] * 3,
        out_specs=(vmem,) * 4,
        scratch_shapes=[
            pltpu.VMEM((device_total, 2, BLK, head_dim), BF16),
            pltpu.VMEM((rows, head_dim), BF16),
            pltpu.VMEM((rows, head_dim), BF16),
            pltpu.VMEM((head_dim, rows), BF16),
            pltpu.VMEM((head_dim, rows), BF16),
            pltpu.VMEM((device_total, rows), F32),
            pltpu.VMEM((BLK, rows), F32),
            pltpu.VMEM((1, rows), F32),
            pltpu.VMEM((1, rows), F32),
            pltpu.VMEM((head_dim, rows), F32),
            pltpu.VMEM((head_dim, rows), F32),
            pltpu.VMEM((device_total, rows), F32),
            pltpu.VMEM((kept, rows), F32),
            pltpu.VMEM((kept, rows), F32),
            pltpu.VMEM((device_total, 2, BLK, head_dim), BF16),
            pltpu.VMEM((x_size * z_size, 2, BLK, head_dim), BF16),
            pltpu.VMEM((max(1, (x_size - 1) * z_size), 2, BLK, head_dim), BF16),
            pltpu.VMEM((max(1, z_size - 1), 2, BLK, head_dim), BF16),
            pltpu.SemaphoreType.DMA((device_total,)),
            pltpu.SemaphoreType.DMA((device_total,)),
            pltpu.SemaphoreType.DMA((device_total,)),
            pltpu.SemaphoreType.DMA((device_total,)),
        ],
        compiler_params=pltpu.CompilerParams(
            collective_id=0, has_side_effects=True, vmem_limit_bytes=48 * 1024 * 1024
        ),
        name="sparse_attention",
    )
    return call(queries, keys, values, grad_out, key_blocks, key_counts, block_slot)


def solution(mesh):
    wide = P(("groups", "ctx"), None)
    return jax.shard_map(
        per_device,
        mesh=mesh,
        in_specs=(wide, wide, wide, wide, P("groups", None), P("groups"), P("groups")),
        out_specs=(wide,) * 4,
        check_vma=False,
    )
```

```python
import functools
import math

import jax
import jax.numpy as jnp
from jax import lax
from jax.experimental import pallas as pl
from jax.experimental.pallas import tpu as pltpu
from jax.sharding import PartitionSpec as P

BLK = 128
NEG = -1e30
F32 = jnp.float32
BF16 = jnp.bfloat16
MESH = pl.DeviceIdType.MESH


def grid_of(device_total):
    chips = device_total // 2
    power = chips.bit_length() - 1
    x_size = 2 ** (power // 3)
    return chips // x_size, x_size


def loop(count, body, most=4):
    if count <= most:
        for step in range(count):
            body(step)
    else:
        lax.fori_loop(0, count, lambda step, _: (body(step), 0)[1], 0)


def dot(a, b, a_dim, b_dim):
    return lax.dot_general(a, b, (((a_dim,), (b_dim,)), ((), ())), preferred_element_type=F32)


def kernel(
    sizes,
    q_hbm, k_hbm, v_hbm, g_hbm, lists_ref, counts_ref, slot_ref,
    out_ref, dq_ref, dk_ref, dv_ref,
    q_ref, g_ref, load_sem, kv, q_rows, g_rows, q_cols, g_cols, bias, tri, top, total, acc, dq_acc, tops,
    exps, dprobs, part, from_core, from_x, from_z,
    ag_send, ag_recv, rs_send, rs_recv,
):
    heads, head_dim, z_size, x_size, keep = sizes
    device_total = 2 * x_size * z_size
    lines = 2 * x_size
    rows = heads * BLK
    scale = 1.0 / math.sqrt(head_dim)
    scale2 = scale * math.log2(math.e)
    me = lax.axis_index("ctx")
    group = lax.axis_index("groups")
    c = lax.rem(me, 2)
    x = lax.rem(me // 2, x_size)
    z = me // (2 * x_size)
    other = 1 - c

    def device(zi, xi, ci):
        return (group, (zi * x_size + xi) * 2 + ci)

    def place(z_step, x_step, c_step):
        return (x_step * 2 + c_step) * z_size + z_step

    def tile(block):
        return pl.ds(pl.multiple_of(block * BLK, BLK), BLK)

    def turn_z(step):
        return lax.rem(z + step, z_size)

    def turn_x(step):
        return lax.rem(x + step, x_size)

    mine = 0
    loads = [
        pltpu.make_async_copy(source, target, load_sem.at[number])
        for number, (source, target) in enumerate((
            (k_hbm, kv.at[0, 0]),
            (v_hbm, kv.at[0, 1]),
            (q_hbm, q_ref),
            (g_hbm, g_ref),
        ))
    ]
    for load in loads:
        load.start()
    barrier = pltpu.get_barrier_semaphore()
    for step in range(1, z_size):
        pl.semaphore_signal(barrier, inc=1, device_id=device(turn_z(step), x, c), device_id_type=MESH)
    for step in range(1, x_size):
        pl.semaphore_signal(barrier, inc=1, device_id=device(z, turn_x(step), c), device_id_type=MESH)
    pl.semaphore_signal(barrier, inc=1, device_id=device(z, x, other), device_id_type=MESH)

    loads[0].wait()
    loads[1].wait()
    pl.semaphore_wait(barrier, z_size + x_size - 1)

    def share(block, there, where, number):
        return pltpu.make_async_remote_copy(
            src_ref=kv.at[block],
            dst_ref=kv.at[there],
            send_sem=ag_send.at[number],
            recv_sem=ag_recv.at[there],
            device_id=where,
            device_id_type=MESH,
        )

    x_base = z_size - 1
    core_base = x_base + (x_size - 1) * z_size

    def share_z(step):
        return share(mine, place(z_size - step, 0, 0), device(turn_z(step), x, c), step - 1)

    def share_x(x_step, z_step):
        return share(
            place(z_step, 0, 0),
            place(z_step, x_size - x_step, 0),
            device(z, turn_x(x_step), c),
            x_base + (x_step - 1) * z_size + z_step,
        )

    def share_core(x_step, z_step):
        return share(
            place(z_step, x_step, 0),
            place(z_step, x_step, 1),
            device(z, x, other),
            core_base + x_step * z_size + z_step,
        )

    loop(x_size - 1, lambda i: share_x(i + 1, 0).start())
    loop(z_size - 1, lambda i: share_z(i + 1).start(), 15)
    share_core(0, 0).start()

    loads[2].wait()
    loads[3].wait()
    for h in range(heads):
        cols = slice(h * head_dim, (h + 1) * head_dim)
        q_tile = q_ref[:, cols]
        g_tile = g_ref[:, cols]
        q_rows[h * BLK:(h + 1) * BLK, :] = q_tile
        g_rows[h * BLK:(h + 1) * BLK, :] = g_tile
        q_cols[:, h * BLK:(h + 1) * BLK] = q_tile.T
        g_cols[:, h * BLK:(h + 1) * BLK] = g_tile.T

    block_total, slot_total = lists_ref.shape

    def find(j, found):
        return jnp.where(slot_ref[j] == me, j, found)

    query_block = lax.fori_loop(0, block_total, find, jnp.int32(0))
    count = counts_ref[query_block]
    bias[...] = jnp.full(bias.shape, NEG, F32)
    block_ids = lax.broadcasted_iota(jnp.int32, bias.shape, 0)

    def open_block(k, _):
        stored = slot_ref[lists_ref[query_block, k]]
        c_step = lax.rem(stored + c, 2)
        x_step = lax.rem(stored // 2 - x + lines, x_size)
        z_step = lax.rem(stored // lines - z + z_size, z_size)
        spot = place(z_step, x_step, c_step)
        spot = jnp.where(k < count, spot, -1)
        bias[...] = jnp.where(block_ids == spot, 0.0, bias[...])
        return 0

    lax.fori_loop(0, slot_total, open_block, 0)
    key_at = lax.broadcasted_iota(jnp.int32, (BLK, rows), 0)
    query_at = lax.rem(lax.broadcasted_iota(jnp.int32, (BLK, rows), 1), BLK)
    tri[...] = jnp.where(key_at <= query_at, 0.0, NEG)
    top[...] = jnp.full(top.shape, NEG, F32)
    total[...] = jnp.zeros(total.shape, F32)
    acc[...] = jnp.zeros(acc.shape, F32)
    dq_acc[...] = jnp.zeros(dq_acc.shape, F32)

    def scores_of(block, own):
        raw = dot(kv[block, 0], q_cols[...], 1, 0) * scale2
        return raw + (tri[...] if own else bias[pl.ds(block, 1), :])

    def forward(block, own=False):
        values = kv[block, 1]
        scores = scores_of(block, own)
        old = top[...]
        new = jnp.maximum(old, jnp.max(scores, axis=0, keepdims=True))
        terms = jnp.exp2(scores - new)
        fade = jnp.exp2(old - new)
        top[...] = new
        total[...] = total[...] * fade + jnp.sum(terms, axis=0, keepdims=True)
        acc[...] = acc[...] * fade + dot(values, terms.astype(BF16), 0, 0)
        if keep:
            exps[tile(block), :] = terms
            tops[pl.ds(block, 1), :] = new
            dprobs[tile(block), :] = dot(values, g_cols[...], 1, 0)

    forward(mine, True)

    def take_z(i):
        step = i + 1
        block = place(step, 0, 0)
        share(mine, block, device(z, x, other), 0).wait_recv()
        loop(x_size - 1, lambda j: share_x(j + 1, step).start())
        share_core(0, step).start()

    loop(z_size - 1, take_z)
    loop(z_size - 1, lambda i: forward(place(i + 1, 0, 0)), 0)

    def take_x(x_step):
        def one(step):
            block = place(step, x_step, 0)
            share(mine, block, device(z, x, other), 0).wait_recv()
            share_core(x_step, step).start()

        loop(z_size, one)
        loop(z_size, lambda step: forward(place(step, x_step, 0)), 0)

    loop(x_size - 1, lambda i: take_x(i + 1))

    def take_core(x_step):
        def one(step):
            block = place(step, x_step, 1)
            share(mine, block, device(z, x, other), 0).wait_recv()
            forward(block)

        loop(z_size, one, 0)

    loop(x_size, take_core, 0)

    inverse = 1.0 / total[...]
    attended = (acc[...] * inverse).T.astype(BF16)
    for h in range(heads):
        part_rows = slice(h * BLK, (h + 1) * BLK)
        out_ref[:, h * head_dim:(h + 1) * head_dim] = attended[part_rows, :]
    rounded = (acc[...] * inverse).astype(BF16).astype(F32)
    delta = jnp.sum(g_cols[...].astype(F32) * rounded, axis=0, keepdims=True)
    total[...] = inverse
    acc[0:1, :] = delta

    def backward(block, own=False):
        keys = kv[block, 0]
        if keep:
            probs = exps[tile(block), :] * (
                jnp.exp2(tops[pl.ds(block, 1), :] - top[...]) * total[...]
            )
            dprob = dprobs[tile(block), :]
        else:
            probs = jnp.exp2(scores_of(block, own) - top[...]) * total[...]
            dprob = dot(kv[block, 1], g_cols[...], 1, 0)
        dscores = (probs * (dprob - acc[0:1, :])).astype(BF16)
        dq_acc[...] += dot(keys, dscores, 0, 0)
        dkey = dot(dscores, q_rows[...], 1, 0) * scale
        dvalue = dot(probs.astype(BF16), g_rows[...], 1, 0)
        return dkey, dvalue

    def post(block, pair):
        part[block, 0] = pair[0].astype(BF16)
        part[block, 1] = pair[1].astype(BF16)

    def plus(pair, landed, slot):
        return (
            pair[0] + landed[slot, 0].astype(F32),
            pair[1] + landed[slot, 1].astype(F32),
        )

    def give(block, landed, slot, where, number):
        return pltpu.make_async_remote_copy(
            src_ref=part.at[block],
            dst_ref=landed.at[slot],
            send_sem=rs_send.at[number],
            recv_sem=rs_recv.at[number],
            device_id=where,
            device_id_type=MESH,
        )

    def give_core(x_at, z_at):
        slot = x_at * z_size + z_at
        return give(
            place(z_at, x_at, 1), from_core, slot, device(z, x, other), core_base + slot
        )

    def give_x(x_step, z_at):
        slot = (x_step - 1) * z_size + z_at
        return give(
            place(z_at, x_step, 0), from_x, slot, device(z, turn_x(x_step), c), x_base + slot
        )

    def give_z(z_step):
        return give(
            place(z_step, 0, 0), from_z, z_step - 1, device(turn_z(z_step), x, c), z_step - 1
        )

    def one_to_core(x_at, z_at):
        block = place(z_at, x_at, 1)
        post(block, backward(block))
        give_core(x_at, z_at).start()

    def one_to_x(x_step, z_at):
        block = place(z_at, x_step, 0)
        pair = backward(block)
        give_core(x_step, z_at).wait_recv()
        post(block, plus(pair, from_core, x_step * z_size + z_at))
        give_x(x_step, z_at).start()

    def away(i):
        x_step = i + 1
        one_to_core(x_step, 1 % z_size)

        def both(j):
            one_to_core(x_step, lax.rem(j + 2, z_size))
            one_to_x(x_step, j + 1)

        loop(z_size - 1, both, 0)
        one_to_x(x_step, 0)

    loop(x_size - 1, away, 1)
    loop(z_size, lambda j: one_to_core(0, lax.rem(j + 1, z_size)), 0)

    def gathered(z_at, own):
        block = place(z_at, 0, 0)
        pair = backward(block, own)
        give_core(0, z_at).wait_recv()
        pair = plus(pair, from_core, z_at)
        for x_step in range(1, x_size):
            give_x(x_step, z_at).wait_recv()
            pair = plus(pair, from_x, (x_step - 1) * z_size + z_at)
        return block, pair

    def to_z(i):
        block, pair = gathered(i + 1, False)
        post(block, pair)
        give_z(i + 1).start()

    loop(z_size - 1, to_z, 0)
    block, pair = gathered(0, True)
    query_grad = (dq_acc[...] * scale).T.astype(BF16)
    for h in range(heads):
        dq_ref[:, h * head_dim:(h + 1) * head_dim] = query_grad[h * BLK:(h + 1) * BLK, :]
    for z_step in range(1, z_size):
        give_z(z_step).wait_recv()
        pair = plus(pair, from_z, z_step - 1)
    dk_ref[...] = pair[0].astype(BF16)
    dv_ref[...] = pair[1].astype(BF16)

    loop(device_total - 1, lambda i: share(mine, mine, device(z, x, other), i).wait_send(), 0)
    loop(
        device_total - 1,
        lambda i: give(mine, from_core, 0, device(z, x, other), i).wait_send(),
        0,
    )


def per_device(queries, keys, values, grad_out, key_blocks, key_counts, block_slot):
    token_rows, width = queries.shape
    head_dim = keys.shape[1]
    heads = width // head_dim
    device_total = key_blocks.shape[0] * BLK // token_rows
    z_size, x_size = grid_of(device_total)
    keep = device_total <= 32
    rows = heads * BLK
    kept = device_total * BLK if keep else 8
    vmem = pl.BlockSpec(memory_space=pltpu.VMEM)
    smem = pl.BlockSpec(memory_space=pltpu.SMEM)
    call = pl.pallas_call(
        functools.partial(kernel, (heads, head_dim, z_size, x_size, keep)),
        out_shape=(
            jax.ShapeDtypeStruct(queries.shape, BF16),
            jax.ShapeDtypeStruct(queries.shape, BF16),
            jax.ShapeDtypeStruct(keys.shape, BF16),
            jax.ShapeDtypeStruct(values.shape, BF16),
        ),
        in_specs=[pl.BlockSpec(memory_space=pl.ANY)] * 4 + [smem] * 3,
        out_specs=(vmem,) * 4,
        scratch_shapes=[
            pltpu.VMEM(queries.shape, BF16),
            pltpu.VMEM(queries.shape, BF16),
            pltpu.SemaphoreType.DMA((4,)),
            pltpu.VMEM((device_total, 2, BLK, head_dim), BF16),
            pltpu.VMEM((rows, head_dim), BF16),
            pltpu.VMEM((rows, head_dim), BF16),
            pltpu.VMEM((head_dim, rows), BF16),
            pltpu.VMEM((head_dim, rows), BF16),
            pltpu.VMEM((device_total, rows), F32),
            pltpu.VMEM((BLK, rows), F32),
            pltpu.VMEM((1, rows), F32),
            pltpu.VMEM((1, rows), F32),
            pltpu.VMEM((head_dim, rows), F32),
            pltpu.VMEM((head_dim, rows), F32),
            pltpu.VMEM((device_total, rows), F32),
            pltpu.VMEM((kept, rows), F32),
            pltpu.VMEM((kept, rows), F32),
            pltpu.VMEM((device_total, 2, BLK, head_dim), BF16),
            pltpu.VMEM((x_size * z_size, 2, BLK, head_dim), BF16),
            pltpu.VMEM((max(1, (x_size - 1) * z_size), 2, BLK, head_dim), BF16),
            pltpu.VMEM((max(1, z_size - 1), 2, BLK, head_dim), BF16),
            pltpu.SemaphoreType.DMA((device_total,)),
            pltpu.SemaphoreType.DMA((device_total,)),
            pltpu.SemaphoreType.DMA((device_total,)),
            pltpu.SemaphoreType.DMA((device_total,)),
        ],
        compiler_params=pltpu.CompilerParams(
            collective_id=0, has_side_effects=True, vmem_limit_bytes=48 * 1024 * 1024
        ),
        name="sparse_attention",
    )
    return call(queries, keys, values, grad_out, key_blocks, key_counts, block_slot)


def solution(mesh):
    wide = P(("groups", "ctx"), None)
    return jax.shard_map(
        per_device,
        mesh=mesh,
        in_specs=(wide, wide, wide, wide, P("groups", None), P("groups"), P("groups")),
        out_specs=(wide,) * 4,
        check_vma=False,
    )
```

```python
import functools
import math

import jax
import jax.numpy as jnp
from jax import lax
from jax.experimental import pallas as pl
from jax.experimental.pallas import tpu as pltpu
from jax.sharding import PartitionSpec as P

BLK = 128
NEG = -1e30
F32 = jnp.float32
BF16 = jnp.bfloat16
MESH = pl.DeviceIdType.MESH


def grid_of(device_total):
    chips = device_total // 2
    power = chips.bit_length() - 1
    x_size = 2 ** (power // 3)
    return chips // x_size, x_size


def loop(count, body, most=4):
    if count <= most:
        for step in range(count):
            body(step)
    else:
        lax.fori_loop(0, count, lambda step, _: (body(step), 0)[1], 0)


def dot(a, b, a_dim, b_dim):
    return lax.dot_general(a, b, (((a_dim,), (b_dim,)), ((), ())), preferred_element_type=F32)


def kernel(
    sizes,
    q_hbm, k_hbm, v_hbm, g_hbm, lists_ref, counts_ref, slot_ref,
    out_ref, dq_ref, dk_ref, dv_ref,
    q_ref, g_ref, load_sem, kv, q_rows, g_rows, q_cols, g_cols, bias, tri, top, total, acc, dq_acc, tops,
    exps, dprobs, part, from_core, from_x, from_z,
    ag_send, ag_recv, rs_send, rs_recv,
):
    heads, head_dim, z_size, x_size, keep = sizes
    device_total = 2 * x_size * z_size
    lines = 2 * x_size
    rows = heads * BLK
    scale = 1.0 / math.sqrt(head_dim)
    scale2 = scale * math.log2(math.e)
    me = lax.axis_index("ctx")
    group = lax.axis_index("groups")
    c = lax.rem(me, 2)
    x = lax.rem(me // 2, x_size)
    z = me // (2 * x_size)
    other = 1 - c

    def device(zi, xi, ci):
        return (group, (zi * x_size + xi) * 2 + ci)

    def place(z_step, x_step, c_step):
        return (x_step * 2 + c_step) * z_size + z_step

    def tile(block):
        return pl.ds(pl.multiple_of(block * BLK, BLK), BLK)

    def turn_z(step):
        return lax.rem(z + step, z_size)

    def turn_x(step):
        return lax.rem(x + step, x_size)

    mine = 0
    loads = [
        pltpu.make_async_copy(source, target, load_sem.at[number])
        for number, (source, target) in enumerate((
            (k_hbm, kv.at[0, 0]),
            (v_hbm, kv.at[0, 1]),
            (q_hbm, q_ref),
            (g_hbm, g_ref),
        ))
    ]
    for load in loads:
        load.start()
    barrier = pltpu.get_barrier_semaphore()
    for step in range(1, z_size):
        pl.semaphore_signal(barrier, inc=1, device_id=device(turn_z(step), x, c), device_id_type=MESH)
    for step in range(1, x_size):
        pl.semaphore_signal(barrier, inc=1, device_id=device(z, turn_x(step), c), device_id_type=MESH)
    pl.semaphore_signal(barrier, inc=1, device_id=device(z, x, other), device_id_type=MESH)

    loads[0].wait()
    loads[1].wait()
    pl.semaphore_wait(barrier, z_size + x_size - 1)

    def share(block, there, where, number):
        return pltpu.make_async_remote_copy(
            src_ref=kv.at[block],
            dst_ref=kv.at[there],
            send_sem=ag_send.at[number],
            recv_sem=ag_recv.at[there],
            device_id=where,
            device_id_type=MESH,
        )

    x_base = z_size - 1
    core_base = x_base + (x_size - 1) * z_size

    def share_z(step):
        return share(mine, place(z_size - step, 0, 0), device(turn_z(step), x, c), step - 1)

    def share_x(x_step, z_step):
        return share(
            place(z_step, 0, 0),
            place(z_step, x_size - x_step, 0),
            device(z, turn_x(x_step), c),
            x_base + (x_step - 1) * z_size + z_step,
        )

    def share_core(x_step, z_step):
        return share(
            place(z_step, x_step, 0),
            place(z_step, x_step, 1),
            device(z, x, other),
            core_base + x_step * z_size + z_step,
        )

    loop(x_size - 1, lambda i: share_x(i + 1, 0).start())
    loop(z_size - 1, lambda i: share_z(i + 1).start(), 15)
    share_core(0, 0).start()

    loads[2].wait()
    loads[3].wait()
    for h in range(heads):
        cols = slice(h * head_dim, (h + 1) * head_dim)
        q_tile = q_ref[:, cols]
        g_tile = g_ref[:, cols]
        q_rows[h * BLK:(h + 1) * BLK, :] = q_tile
        g_rows[h * BLK:(h + 1) * BLK, :] = g_tile
        q_cols[:, h * BLK:(h + 1) * BLK] = q_tile.T
        g_cols[:, h * BLK:(h + 1) * BLK] = g_tile.T

    block_total, slot_total = lists_ref.shape

    def find(j, found):
        return jnp.where(slot_ref[j] == me, j, found)

    query_block = lax.fori_loop(0, block_total, find, jnp.int32(0))
    count = counts_ref[query_block]
    bias[...] = jnp.full(bias.shape, NEG, F32)
    block_ids = lax.broadcasted_iota(jnp.int32, bias.shape, 0)

    def open_block(k, _):
        stored = slot_ref[lists_ref[query_block, k]]
        c_step = lax.rem(stored + c, 2)
        x_step = lax.rem(stored // 2 - x + lines, x_size)
        z_step = lax.rem(stored // lines - z + z_size, z_size)
        spot = place(z_step, x_step, c_step)
        spot = jnp.where(k < count, spot, -1)
        bias[...] = jnp.where(block_ids == spot, 0.0, bias[...])
        return 0

    lax.fori_loop(0, slot_total, open_block, 0)
    key_at = lax.broadcasted_iota(jnp.int32, (BLK, rows), 0)
    query_at = lax.rem(lax.broadcasted_iota(jnp.int32, (BLK, rows), 1), BLK)
    tri[...] = jnp.where(key_at <= query_at, 0.0, NEG)
    top[...] = jnp.full(top.shape, NEG, F32)
    total[...] = jnp.zeros(total.shape, F32)
    acc[...] = jnp.zeros(acc.shape, F32)
    dq_acc[...] = jnp.zeros(dq_acc.shape, F32)

    def scores_of(block, own):
        raw = dot(kv[block, 0], q_cols[...], 1, 0) * scale2
        return raw + (tri[...] if own else bias[pl.ds(block, 1), :])

    def forward(block, own=False):
        values = kv[block, 1]
        scores = scores_of(block, own)
        old = top[...]
        new = jnp.maximum(old, jnp.max(scores, axis=0, keepdims=True))
        terms = jnp.exp2(scores - new)
        fade = jnp.exp2(old - new)
        top[...] = new
        total[...] = total[...] * fade + jnp.sum(terms, axis=0, keepdims=True)
        acc[...] = acc[...] * fade + dot(values, terms.astype(BF16), 0, 0)
        if keep:
            exps[tile(block), :] = terms
            tops[pl.ds(block, 1), :] = new
            dprobs[tile(block), :] = dot(values, g_cols[...], 1, 0)

    forward(mine, True)

    def take_z(i):
        step = i + 1
        block = place(step, 0, 0)
        share(mine, block, device(z, x, other), 0).wait_recv()
        loop(x_size - 1, lambda j: share_x(j + 1, step).start())
        share_core(0, step).start()

    loop(z_size - 1, take_z)
    loop(z_size - 1, lambda i: forward(place(i + 1, 0, 0)), 0)

    def take_x(x_step):
        def one(step):
            block = place(step, x_step, 0)
            share(mine, block, device(z, x, other), 0).wait_recv()
            share_core(x_step, step).start()

        loop(z_size, one)
        loop(z_size, lambda step: forward(place(step, x_step, 0)), 0)

    loop(x_size - 1, lambda i: take_x(i + 1))

    def take_core(x_step):
        def one(step):
            block = place(step, x_step, 1)
            share(mine, block, device(z, x, other), 0).wait_recv()
            forward(block)

        loop(z_size, one, 0)

    loop(x_size, take_core, 0)

    inverse = 1.0 / total[...]
    attended = (acc[...] * inverse).T.astype(BF16)
    for h in range(heads):
        part_rows = slice(h * BLK, (h + 1) * BLK)
        out_ref[:, h * head_dim:(h + 1) * head_dim] = attended[part_rows, :]
    rounded = (acc[...] * inverse).astype(BF16).astype(F32)
    delta = jnp.sum(g_cols[...].astype(F32) * rounded, axis=0, keepdims=True)
    total[...] = inverse
    acc[0:1, :] = delta

    def backward(block, own=False):
        keys = kv[block, 0]
        if keep:
            probs = exps[tile(block), :] * (
                jnp.exp2(tops[pl.ds(block, 1), :] - top[...]) * total[...]
            )
            dprob = dprobs[tile(block), :]
        else:
            probs = jnp.exp2(scores_of(block, own) - top[...]) * total[...]
            dprob = dot(kv[block, 1], g_cols[...], 1, 0)
        dscores = (probs * (dprob - acc[0:1, :])).astype(BF16)
        dq_acc[...] += dot(keys, dscores, 0, 0)
        dkey = dot(dscores, q_rows[...], 1, 0) * scale
        dvalue = dot(probs.astype(BF16), g_rows[...], 1, 0)
        return dkey, dvalue

    def post(block, pair):
        part[block, 0] = pair[0].astype(BF16)
        part[block, 1] = pair[1].astype(BF16)

    def plus(pair, landed, slot):
        return (
            pair[0] + landed[slot, 0].astype(F32),
            pair[1] + landed[slot, 1].astype(F32),
        )

    def give(block, landed, slot, where, number):
        return pltpu.make_async_remote_copy(
            src_ref=part.at[block],
            dst_ref=landed.at[slot],
            send_sem=rs_send.at[number],
            recv_sem=rs_recv.at[number],
            device_id=where,
            device_id_type=MESH,
        )

    def give_core(x_at, z_at):
        slot = x_at * z_size + z_at
        return give(
            place(z_at, x_at, 1), from_core, slot, device(z, x, other), core_base + slot
        )

    def give_x(x_step, z_at):
        slot = (x_step - 1) * z_size + z_at
        return give(
            place(z_at, x_step, 0), from_x, slot, device(z, turn_x(x_step), c), x_base + slot
        )

    def give_z(z_step):
        return give(
            place(z_step, 0, 0), from_z, z_step - 1, device(turn_z(z_step), x, c), z_step - 1
        )

    def one_to_core(x_at, z_at):
        block = place(z_at, x_at, 1)
        post(block, backward(block))
        give_core(x_at, z_at).start()

    def one_to_x(x_step, z_at):
        block = place(z_at, x_step, 0)
        pair = backward(block)
        give_core(x_step, z_at).wait_recv()
        post(block, plus(pair, from_core, x_step * z_size + z_at))
        give_x(x_step, z_at).start()

    def away(i):
        x_step = i + 1
        one_to_core(x_step, 1 % z_size)

        def both(j):
            one_to_core(x_step, lax.rem(j + 2, z_size))
            one_to_x(x_step, j + 1)

        loop(z_size - 1, both, 0)
        one_to_x(x_step, 0)

    loop(x_size - 1, away, 1)
    loop(z_size, lambda j: one_to_core(0, lax.rem(j + 1, z_size)), 0)

    def gathered(z_at, own):
        block = place(z_at, 0, 0)
        pair = backward(block, own)
        give_core(0, z_at).wait_recv()
        pair = plus(pair, from_core, z_at)
        for x_step in range(1, x_size):
            give_x(x_step, z_at).wait_recv()
            pair = plus(pair, from_x, (x_step - 1) * z_size + z_at)
        return block, pair

    def to_z(i):
        block, pair = gathered(i + 1, False)
        post(block, pair)
        give_z(i + 1).start()

    loop(z_size - 1, to_z, 0)
    block, pair = gathered(0, True)
    query_grad = (dq_acc[...] * scale).T.astype(BF16)
    for h in range(heads):
        dq_ref[:, h * head_dim:(h + 1) * head_dim] = query_grad[h * BLK:(h + 1) * BLK, :]
    for z_step in range(1, z_size):
        give_z(z_step).wait_recv()
        pair = plus(pair, from_z, z_step - 1)
    dk_ref[...] = pair[0].astype(BF16)
    dv_ref[...] = pair[1].astype(BF16)

    loop(device_total - 1, lambda i: share(mine, mine, device(z, x, other), i).wait_send(), 0)
    loop(
        device_total - 1,
        lambda i: give(mine, from_core, 0, device(z, x, other), i).wait_send(),
        0,
    )


def store_kernel(*refs):
    sources, targets, sem = refs[:4], refs[4:8], refs[8]
    copies = [
        pltpu.make_async_copy(source, target, sem.at[number])
        for number, (source, target) in enumerate(zip(sources, targets))
    ]
    for copy in copies:
        copy.start()
    for copy in copies:
        copy.wait()


def per_device(queries, keys, values, grad_out, key_blocks, key_counts, block_slot):
    token_rows, width = queries.shape
    head_dim = keys.shape[1]
    heads = width // head_dim
    device_total = key_blocks.shape[0] * BLK // token_rows
    z_size, x_size = grid_of(device_total)
    keep = device_total <= 32
    rows = heads * BLK
    kept = device_total * BLK if keep else 8
    vmem = pl.BlockSpec(memory_space=pltpu.VMEM)
    smem = pl.BlockSpec(memory_space=pltpu.SMEM)
    call = pl.pallas_call(
        functools.partial(kernel, (heads, head_dim, z_size, x_size, keep)),
        out_shape=(
            jax.ShapeDtypeStruct(queries.shape, BF16),
            jax.ShapeDtypeStruct(queries.shape, BF16),
            jax.ShapeDtypeStruct(keys.shape, BF16),
            jax.ShapeDtypeStruct(values.shape, BF16),
        ),
        in_specs=[pl.BlockSpec(memory_space=pltpu.HBM)] * 4 + [smem] * 3,
        out_specs=(vmem,) * 4,
        scratch_shapes=[
            pltpu.VMEM(queries.shape, BF16),
            pltpu.VMEM(queries.shape, BF16),
            pltpu.SemaphoreType.DMA((4,)),
            pltpu.VMEM((device_total, 2, BLK, head_dim), BF16),
            pltpu.VMEM((rows, head_dim), BF16),
            pltpu.VMEM((rows, head_dim), BF16),
            pltpu.VMEM((head_dim, rows), BF16),
            pltpu.VMEM((head_dim, rows), BF16),
            pltpu.VMEM((device_total, rows), F32),
            pltpu.VMEM((BLK, rows), F32),
            pltpu.VMEM((1, rows), F32),
            pltpu.VMEM((1, rows), F32),
            pltpu.VMEM((head_dim, rows), F32),
            pltpu.VMEM((head_dim, rows), F32),
            pltpu.VMEM((device_total, rows), F32),
            pltpu.VMEM((kept, rows), F32),
            pltpu.VMEM((kept, rows), F32),
            pltpu.VMEM((device_total, 2, BLK, head_dim), BF16),
            pltpu.VMEM((x_size * z_size, 2, BLK, head_dim), BF16),
            pltpu.VMEM((max(1, (x_size - 1) * z_size), 2, BLK, head_dim), BF16),
            pltpu.VMEM((max(1, z_size - 1), 2, BLK, head_dim), BF16),
            pltpu.SemaphoreType.DMA((device_total,)),
            pltpu.SemaphoreType.DMA((device_total,)),
            pltpu.SemaphoreType.DMA((device_total,)),
            pltpu.SemaphoreType.DMA((device_total,)),
        ],
        compiler_params=pltpu.CompilerParams(
            collective_id=0, has_side_effects=True, vmem_limit_bytes=63 * 1024 * 1024
        ),
        name="sparse_attention",
    )
    results = call(queries, keys, values, grad_out, key_blocks, key_counts, block_slot)
    return pl.pallas_call(
        store_kernel,
        out_shape=tuple(jax.ShapeDtypeStruct(r.shape, r.dtype) for r in results),
        in_specs=[pl.BlockSpec(memory_space=pl.ANY)] * 4,
        out_specs=(pl.BlockSpec(memory_space=pltpu.HBM),) * 4,
        scratch_shapes=[pltpu.SemaphoreType.DMA((4,))],
        compiler_params=pltpu.CompilerParams(vmem_limit_bytes=63 * 1024 * 1024),
        name="store_results",
    )(*results)


def solution(mesh):
    wide = P(("groups", "ctx"), None)
    return jax.shard_map(
        per_device,
        mesh=mesh,
        in_specs=(wide, wide, wide, wide, P("groups", None), P("groups"), P("groups")),
        out_specs=(wide,) * 4,
        check_vma=False,
    )
```

```python
import functools
import math

import jax
import jax.numpy as jnp
from jax import lax
from jax.experimental import pallas as pl
from jax.experimental.pallas import tpu as pltpu
from jax.sharding import PartitionSpec as P

BLK = 128
NEG = -1e30
F32 = jnp.float32
BF16 = jnp.bfloat16
MESH = pl.DeviceIdType.MESH


def grid_of(device_total):
    chips = device_total // 2
    power = chips.bit_length() - 1
    x_size = 2 ** (power // 3)
    return chips // x_size, x_size


def loop(count, body, most=4):
    if count <= most:
        for step in range(count):
            body(step)
    else:
        lax.fori_loop(0, count, lambda step, _: (body(step), 0)[1], 0)


def dot(a, b, a_dim, b_dim):
    return lax.dot_general(a, b, (((a_dim,), (b_dim,)), ((), ())), preferred_element_type=F32)


def kernel(
    sizes,
    q_hbm, k_hbm, v_hbm, g_hbm, lists_ref, counts_ref, slot_ref,
    out_ref, dq_ref, dk_ref, dv_ref,
    q_ref, g_ref, load_sem, kv, q_rows, g_rows, q_cols, g_cols, bias, tri, top, total, acc, dq_acc, tops,
    exps, dprobs, part, from_core, from_x, from_z,
    ag_send, ag_recv, rs_send, rs_recv,
):
    heads, head_dim, z_size, x_size, keep = sizes
    device_total = 2 * x_size * z_size
    lines = 2 * x_size
    rows = heads * BLK
    scale = 1.0 / math.sqrt(head_dim)
    scale2 = scale * math.log2(math.e)
    me = lax.axis_index("ctx")
    group = lax.axis_index("groups")
    c = lax.rem(me, 2)
    x = lax.rem(me // 2, x_size)
    z = me // (2 * x_size)
    other = 1 - c

    def device(zi, xi, ci):
        return (group, (zi * x_size + xi) * 2 + ci)

    def place(z_step, x_step, c_step):
        return (x_step * 2 + c_step) * z_size + z_step

    def tile(block):
        return pl.ds(pl.multiple_of(block * BLK, BLK), BLK)

    def turn_z(step):
        return lax.rem(z + step, z_size)

    def turn_x(step):
        return lax.rem(x + step, x_size)

    mine = 0
    loads = [
        pltpu.make_async_copy(source, target, load_sem.at[number])
        for number, (source, target) in enumerate((
            (k_hbm, kv.at[0, 0]),
            (v_hbm, kv.at[0, 1]),
            (q_hbm, q_ref),
            (g_hbm, g_ref),
        ))
    ]
    for load in loads:
        load.start()
    barrier = pltpu.get_barrier_semaphore()
    for step in range(1, z_size):
        pl.semaphore_signal(barrier, inc=1, device_id=device(turn_z(step), x, c), device_id_type=MESH)
    for step in range(1, x_size):
        pl.semaphore_signal(barrier, inc=1, device_id=device(z, turn_x(step), c), device_id_type=MESH)
    pl.semaphore_signal(barrier, inc=1, device_id=device(z, x, other), device_id_type=MESH)

    loads[0].wait()
    loads[1].wait()
    pl.semaphore_wait(barrier, z_size + x_size - 1)

    def share(block, there, where, number):
        return pltpu.make_async_remote_copy(
            src_ref=kv.at[block],
            dst_ref=kv.at[there],
            send_sem=ag_send.at[number],
            recv_sem=ag_recv.at[there],
            device_id=where,
            device_id_type=MESH,
        )

    x_base = z_size - 1
    core_base = x_base + (x_size - 1) * z_size

    def share_z(step):
        return share(mine, place(z_size - step, 0, 0), device(turn_z(step), x, c), step - 1)

    def share_x(x_step, z_step):
        return share(
            place(z_step, 0, 0),
            place(z_step, x_size - x_step, 0),
            device(z, turn_x(x_step), c),
            x_base + (x_step - 1) * z_size + z_step,
        )

    def share_core(x_step, z_step):
        return share(
            place(z_step, x_step, 0),
            place(z_step, x_step, 1),
            device(z, x, other),
            core_base + x_step * z_size + z_step,
        )

    loop(x_size - 1, lambda i: share_x(i + 1, 0).start())
    loop(z_size - 1, lambda i: share_z(i + 1).start(), 15)
    share_core(0, 0).start()

    loads[2].wait()
    loads[3].wait()
    for h in range(heads):
        cols = slice(h * head_dim, (h + 1) * head_dim)
        q_tile = q_ref[:, cols]
        g_tile = g_ref[:, cols]
        q_rows[h * BLK:(h + 1) * BLK, :] = q_tile
        g_rows[h * BLK:(h + 1) * BLK, :] = g_tile
        q_cols[:, h * BLK:(h + 1) * BLK] = q_tile.T
        g_cols[:, h * BLK:(h + 1) * BLK] = g_tile.T

    block_total, slot_total = lists_ref.shape

    def find(j, found):
        return jnp.where(slot_ref[j] == me, j, found)

    query_block = lax.fori_loop(0, block_total, find, jnp.int32(0))
    count = counts_ref[query_block]
    bias[...] = jnp.full(bias.shape, NEG, F32)
    block_ids = lax.broadcasted_iota(jnp.int32, bias.shape, 0)

    def open_block(k, _):
        stored = slot_ref[lists_ref[query_block, k]]
        c_step = lax.rem(stored + c, 2)
        x_step = lax.rem(stored // 2 - x + lines, x_size)
        z_step = lax.rem(stored // lines - z + z_size, z_size)
        spot = place(z_step, x_step, c_step)
        spot = jnp.where(k < count, spot, -1)
        bias[...] = jnp.where(block_ids == spot, 0.0, bias[...])
        return 0

    lax.fori_loop(0, slot_total, open_block, 0)
    key_at = lax.broadcasted_iota(jnp.int32, (BLK, rows), 0)
    query_at = lax.rem(lax.broadcasted_iota(jnp.int32, (BLK, rows), 1), BLK)
    tri[...] = jnp.where(key_at <= query_at, 0.0, NEG)
    top[...] = jnp.full(top.shape, NEG, F32)
    total[...] = jnp.zeros(total.shape, F32)
    acc[...] = jnp.zeros(acc.shape, F32)
    dq_acc[...] = jnp.zeros(dq_acc.shape, F32)

    def scores_of(block, own):
        raw = dot(kv[block, 0], q_cols[...], 1, 0) * scale2
        return raw + (tri[...] if own else bias[pl.ds(block, 1), :])

    def forward(block, own=False):
        values = kv[block, 1]
        scores = scores_of(block, own)
        old = top[...]
        new = jnp.maximum(old, jnp.max(scores, axis=0, keepdims=True))
        terms = jnp.exp2(scores - new)
        fade = jnp.exp2(old - new)
        top[...] = new
        total[...] = total[...] * fade + jnp.sum(terms, axis=0, keepdims=True)
        acc[...] = acc[...] * fade + dot(values, terms.astype(BF16), 0, 0)
        if keep:
            exps[tile(block), :] = terms
            tops[pl.ds(block, 1), :] = new
            dprobs[tile(block), :] = dot(values, g_cols[...], 1, 0)

    forward(mine, True)

    def take_z(i):
        step = i + 1
        block = place(step, 0, 0)
        share(mine, block, device(z, x, other), 0).wait_recv()
        loop(x_size - 1, lambda j: share_x(j + 1, step).start())
        share_core(0, step).start()

    loop(z_size - 1, take_z)
    loop(z_size - 1, lambda i: forward(place(i + 1, 0, 0)), 0)

    def take_x(x_step):
        def one(step):
            block = place(step, x_step, 0)
            share(mine, block, device(z, x, other), 0).wait_recv()
            share_core(x_step, step).start()

        loop(z_size, one)
        loop(z_size, lambda step: forward(place(step, x_step, 0)), 0)

    loop(x_size - 1, lambda i: take_x(i + 1))

    def take_core(x_step):
        def one(step):
            block = place(step, x_step, 1)
            share(mine, block, device(z, x, other), 0).wait_recv()
            forward(block)

        loop(z_size, one, 0)

    loop(x_size, take_core, 0)

    inverse = 1.0 / total[...]
    attended = (acc[...] * inverse).T.astype(BF16)
    for h in range(heads):
        part_rows = slice(h * BLK, (h + 1) * BLK)
        out_ref[:, h * head_dim:(h + 1) * head_dim] = attended[part_rows, :]
    rounded = (acc[...] * inverse).astype(BF16).astype(F32)
    delta = jnp.sum(g_cols[...].astype(F32) * rounded, axis=0, keepdims=True)
    total[...] = inverse
    acc[0:1, :] = delta

    def backward(block, own=False):
        keys = kv[block, 0]
        if keep:
            probs = exps[tile(block), :] * (
                jnp.exp2(tops[pl.ds(block, 1), :] - top[...]) * total[...]
            )
            dprob = dprobs[tile(block), :]
        else:
            probs = jnp.exp2(scores_of(block, own) - top[...]) * total[...]
            dprob = dot(kv[block, 1], g_cols[...], 1, 0)
        dscores = (probs * (dprob - acc[0:1, :])).astype(BF16)
        dq_acc[...] += dot(keys, dscores, 0, 0)
        dkey = dot(dscores, q_rows[...], 1, 0) * scale
        dvalue = dot(probs.astype(BF16), g_rows[...], 1, 0)
        return dkey, dvalue

    def post(block, pair):
        part[block, 0] = pair[0].astype(BF16)
        part[block, 1] = pair[1].astype(BF16)

    def plus(pair, landed, slot):
        return (
            pair[0] + landed[slot, 0].astype(F32),
            pair[1] + landed[slot, 1].astype(F32),
        )

    def give(block, landed, slot, where, number):
        return pltpu.make_async_remote_copy(
            src_ref=part.at[block],
            dst_ref=landed.at[slot],
            send_sem=rs_send.at[number],
            recv_sem=rs_recv.at[number],
            device_id=where,
            device_id_type=MESH,
        )

    def give_core(x_at, z_at):
        slot = x_at * z_size + z_at
        return give(
            place(z_at, x_at, 1), from_core, slot, device(z, x, other), core_base + slot
        )

    def give_x(x_step, z_at):
        slot = (x_step - 1) * z_size + z_at
        return give(
            place(z_at, x_step, 0), from_x, slot, device(z, turn_x(x_step), c), x_base + slot
        )

    def give_z(z_step):
        return give(
            place(z_step, 0, 0), from_z, z_step - 1, device(turn_z(z_step), x, c), z_step - 1
        )

    def one_to_core(x_at, z_at):
        block = place(z_at, x_at, 1)
        post(block, backward(block))
        give_core(x_at, z_at).start()

    def one_to_x(x_step, z_at):
        block = place(z_at, x_step, 0)
        pair = backward(block)
        give_core(x_step, z_at).wait_recv()
        post(block, plus(pair, from_core, x_step * z_size + z_at))
        give_x(x_step, z_at).start()

    def away(i):
        x_step = i + 1
        one_to_core(x_step, 1 % z_size)

        def both(j):
            one_to_core(x_step, lax.rem(j + 2, z_size))
            one_to_x(x_step, j + 1)

        loop(z_size - 1, both, 0)
        one_to_x(x_step, 0)

    loop(x_size - 1, away, 1)
    loop(z_size, lambda j: one_to_core(0, lax.rem(j + 1, z_size)), 0)

    def gathered(z_at, own):
        block = place(z_at, 0, 0)
        pair = backward(block, own)
        give_core(0, z_at).wait_recv()
        pair = plus(pair, from_core, z_at)
        for x_step in range(1, x_size):
            give_x(x_step, z_at).wait_recv()
            pair = plus(pair, from_x, (x_step - 1) * z_size + z_at)
        return block, pair

    def to_z(i):
        block, pair = gathered(i + 1, False)
        post(block, pair)
        give_z(i + 1).start()

    loop(z_size - 1, to_z, 0)
    block, pair = gathered(0, True)
    query_grad = (dq_acc[...] * scale).T.astype(BF16)
    for h in range(heads):
        dq_ref[:, h * head_dim:(h + 1) * head_dim] = query_grad[h * BLK:(h + 1) * BLK, :]
    for z_step in range(1, z_size):
        give_z(z_step).wait_recv()
        pair = plus(pair, from_z, z_step - 1)
    dk_ref[...] = pair[0].astype(BF16)
    dv_ref[...] = pair[1].astype(BF16)

    loop(device_total - 1, lambda i: share(mine, mine, device(z, x, other), i).wait_send(), 0)
    loop(
        device_total - 1,
        lambda i: give(mine, from_core, 0, device(z, x, other), i).wait_send(),
        0,
    )


def store_kernel(*refs):
    for source, target in zip(refs[:4], refs[4:]):
        target[...] = source[...]


def per_device(queries, keys, values, grad_out, key_blocks, key_counts, block_slot):
    token_rows, width = queries.shape
    head_dim = keys.shape[1]
    heads = width // head_dim
    device_total = key_blocks.shape[0] * BLK // token_rows
    z_size, x_size = grid_of(device_total)
    keep = device_total <= 32
    rows = heads * BLK
    kept = device_total * BLK if keep else 8
    vmem = pl.BlockSpec(memory_space=pltpu.VMEM)
    smem = pl.BlockSpec(memory_space=pltpu.SMEM)
    call = pl.pallas_call(
        functools.partial(kernel, (heads, head_dim, z_size, x_size, keep)),
        out_shape=(
            jax.ShapeDtypeStruct(queries.shape, BF16),
            jax.ShapeDtypeStruct(queries.shape, BF16),
            jax.ShapeDtypeStruct(keys.shape, BF16),
            jax.ShapeDtypeStruct(values.shape, BF16),
        ),
        in_specs=[pl.BlockSpec(memory_space=pltpu.HBM)] * 4 + [smem] * 3,
        out_specs=(vmem,) * 4,
        scratch_shapes=[
            pltpu.VMEM(queries.shape, BF16),
            pltpu.VMEM(queries.shape, BF16),
            pltpu.SemaphoreType.DMA((4,)),
            pltpu.VMEM((device_total, 2, BLK, head_dim), BF16),
            pltpu.VMEM((rows, head_dim), BF16),
            pltpu.VMEM((rows, head_dim), BF16),
            pltpu.VMEM((head_dim, rows), BF16),
            pltpu.VMEM((head_dim, rows), BF16),
            pltpu.VMEM((device_total, rows), F32),
            pltpu.VMEM((BLK, rows), F32),
            pltpu.VMEM((1, rows), F32),
            pltpu.VMEM((1, rows), F32),
            pltpu.VMEM((head_dim, rows), F32),
            pltpu.VMEM((head_dim, rows), F32),
            pltpu.VMEM((device_total, rows), F32),
            pltpu.VMEM((kept, rows), F32),
            pltpu.VMEM((kept, rows), F32),
            pltpu.VMEM((device_total, 2, BLK, head_dim), BF16),
            pltpu.VMEM((x_size * z_size, 2, BLK, head_dim), BF16),
            pltpu.VMEM((max(1, (x_size - 1) * z_size), 2, BLK, head_dim), BF16),
            pltpu.VMEM((max(1, z_size - 1), 2, BLK, head_dim), BF16),
            pltpu.SemaphoreType.DMA((device_total,)),
            pltpu.SemaphoreType.DMA((device_total,)),
            pltpu.SemaphoreType.DMA((device_total,)),
            pltpu.SemaphoreType.DMA((device_total,)),
        ],
        compiler_params=pltpu.CompilerParams(
            collective_id=0, has_side_effects=True, vmem_limit_bytes=63 * 1024 * 1024
        ),
        name="sparse_attention",
    )
    results = call(queries, keys, values, grad_out, key_blocks, key_counts, block_slot)
    return pl.pallas_call(
        store_kernel,
        out_shape=tuple(jax.ShapeDtypeStruct(r.shape, r.dtype) for r in results),
        in_specs=[vmem] * 4,
        out_specs=(vmem,) * 4,
        compiler_params=pltpu.CompilerParams(vmem_limit_bytes=63 * 1024 * 1024),
        name="store_results",
    )(*results)


def solution(mesh):
    wide = P(("groups", "ctx"), None)
    return jax.shard_map(
        per_device,
        mesh=mesh,
        in_specs=(wide, wide, wide, wide, P("groups", None), P("groups"), P("groups")),
        out_specs=(wide,) * 4,
        check_vma=False,
    )
```
